256 devices in a mesh: series: 64 (over z_hi, y, x, core), tick: 4 (over z_lo).
Axes of the slice: x: 4, y: 4, z: 8 (z_hi: 2, z_lo: 4; z = z_hi * 4 + z_lo), core: 2. Of those that a mesh axis runs over, the one named last changes fastest.
Arguments:
- telemetry: float32 [32768, 1024], P('series', 'tick'), may hold values from -81 to 81
- sparse: float32 [32768, 1024], P('series', 'tick'), may hold values from -4 to 4
- multiplier: float32 [32768, 1024], P('series', 'tick'), may hold values from -4 to 4
Outputs:
- lowrank: float32 [32768, 1024], P('series', 'tick')
- new_sparse: float32 [32768, 1024], P('series', 'tick')
- new_multiplier: float32 [32768, 1024], P('series', 'tick')
The draws below stay inside these ranges and needn't reach their ends.
All inputs are finite; a program needn't handle non-finite values.
Results may differ from the reference program's by a relative error of at most 0.0003.
Values sent between devices are 32-bit elements; how exact they have to be, the bound alone decides.
A program may use at most 64 MiB of HBM per device.

```python
import math
import jax
import jax.numpy as jnp
from jax import lax

TICKS = 1024
SERIES = 32768


def draw_telemetry(key, part):
    key = jax.random.fold_in(key, 7)
    noise_key, col_key, row_key = jax.random.split(key, 3)
    position = jnp.arange(TICKS, dtype=jnp.float32) / TICKS
    col_scale = jnp.power(3.0, position) * jnp.exp(jax.random.uniform(col_key, (TICKS,), jnp.float32, 0.0, math.log(4.0)))
    row_scale = jnp.exp(jax.random.uniform(row_key, (SERIES, 1), jnp.float32, 0.0, math.log(3.0)))
    noise = jax.random.normal(noise_key, (SERIES, TICKS), jnp.float32)
    noise = jnp.clip(noise, -6.0, 6.0)
    return (noise * row_scale * col_scale[None, :] * 0.25).astype(jnp.float32)


def block_scale(rng, dims, pieces, smallest, top_value):
    gain = 1.0
    for dim, blocks in pieces:
        steps = jax.random.uniform(jax.random.fold_in(jax.random.fold_in(rng, 6), dim), (blocks,), jnp.float32, smallest / len(pieces), top_value / len(pieces))
        gain = gain * jnp.repeat(jnp.exp(steps), dims[dim] // blocks).reshape((-1,) + (1,) * (len(dims) - 1 - dim))
    return gain


def centred(stream_key, extent, width, bound, cuts=(), kind=jnp.bfloat16):
    factor_of = block_scale(stream_key, extent, cuts, -0.22, 0.18) if cuts else 1.0
    drawn = jax.random.normal(stream_key, extent, jnp.float32) * width * factor_of
    return jnp.minimum(jnp.maximum(drawn, -bound), bound).astype(kind)


def setup_inputs(seed: int = 0) -> dict:
    key_of = jax.random.split(jax.random.key(seed), 4)
    return {
        "telemetry": draw_telemetry(jax.random.fold_in(key_of[3], 71), 0),
        "sparse": centred(key_of[1], (SERIES, TICKS), 0.5, 4.0, ((0, 64), (1, 4)), jnp.float32),
        "multiplier": centred(key_of[2], (SERIES, TICKS), 0.5, 4.0, ((0, 64), (1, 4)), jnp.float32),
    }


chebyshev_coefs = (0.4, 0.5, 0.1, -0.04, -0.06)
shrink_level = 0.5

def reference(telemetry, sparse, multiplier):
    blended = telemetry - sparse + multiplier
    gram = jnp.dot(blended.T, blended, precision=lax.Precision.HIGHEST, preferred_element_type=jnp.float32)
    frobenius = jnp.sqrt(jnp.sum(gram * gram) + jnp.float32(1e-06))
    factor = 2.0 / frobenius

    def operator(matrix):
        return factor * jnp.dot(matrix, gram, precision=lax.Precision.HIGHEST, preferred_element_type=jnp.float32) - matrix
    earlier = blended
    current = operator(blended)
    lowrank = chebyshev_coefs[0] * earlier + chebyshev_coefs[1] * current
    for degree in range(2, 5):
        following = 2.0 * operator(current) - earlier
        lowrank = lowrank + chebyshev_coefs[degree] * following
        earlier, current = (current, following)
    level = telemetry - lowrank + multiplier
    new_sparse = jnp.sign(level) * jnp.maximum(jnp.abs(level) - shrink_level, 0.0)
    new_multiplier = multiplier + telemetry - lowrank - new_sparse
    return (lowrank, new_sparse, new_multiplier)
```

```python
import functools

import jax
import jax.numpy as jnp
from jax import lax
from jax.experimental import pallas as pl
from jax.experimental.pallas import tpu as pltpu
from jax.sharding import PartitionSpec as P

MESH = pl.DeviceIdType.MESH
coefs = (0.4, 0.5, 0.1, -0.04, -0.06)
shrink_level = 0.5
f32, bf16 = jnp.float32, jnp.bfloat16

pairs = (
    ((0, 0), (0, 1), (0, 2), (0, 3), (1, 1)),
    ((1, 2), (1, 3), (2, 2), (2, 3), (3, 3)),
)


def split(value):
    high = value.astype(bf16)
    return high, (value - high.astype(f32)).astype(bf16)


def dot(a, b, dims=((1,), (0,))):
    return lax.dot_general(a, b, (dims, ((), ())), preferred_element_type=f32)


def kernel(
    tele, sparse, mult, low_out, sparse_out, mult_out,
    wf, wp, gh, gl, part, r1, s1, r2, s2, r3, g2, g1, gf,
    gc, gch, gcl, va, vb, vh, vl, acc, wfh, wfl, ss, rs,
):
    series, t = lax.axis_index("series"), lax.axis_index("tick")
    c = series % 2
    x = (series // 2) % 4
    y = (series // 8) % 4
    zh = series // 32

    def at(zh_, t_, y_, x_, c_):
        return ((zh_ * 4 + y_) * 4 + x_) * 2 + c_, t_

    def xpeer(d):
        return at(zh, t, y, (x + d) % 4, c)

    def ypeer(d):
        return at(zh, t, (y + d) % 4, x, c)

    def zpeer(dh, d):
        return at((zh + dh) % 2, (t + d) % 4, y, x, c)

    partner = at(zh, t, y, x, 1 - c)
    count = [0]

    def send(src, dst, device):
        k = count[0]
        count[0] += 1
        copy = pltpu.make_async_remote_copy(
            src_ref=src, dst_ref=dst, send_sem=ss.at[k], recv_sem=rs.at[k],
            device_id=device, device_id_type=MESH,
        )
        copy.start()
        return copy

    sent = []

    barrier = pltpu.get_barrier_semaphore()
    peers = [xpeer(d) for d in (1, 2, 3)] + [ypeer(d) for d in (1, 2, 3)]
    peers += [zpeer(dh, d) for dh in (0, 1) for d in range(4) if dh or d] + [partner]
    for p in peers:
        pl.semaphore_signal(barrier, inc=1, device_id=p, device_id_type=MESH)
    wf[t] = tele[...] - sparse[...] + mult[...]
    pl.semaphore_wait(barrier, len(peers))

    first = []
    for d in (1, 2, 3):
        q = (t + d) % 4
        block = wf.at[t, pl.ds(128 * q, 128)]
        first.append(send(block, block, zpeer(0, d)))
    mine = pl.ds(pl.multiple_of(128 * t, 128), 128)
    passed = [send(wf.at[t, mine], wp.at[t], partner)]
    for d in (1, 2, 3):
        first[d - 1].wait_recv()
        o = (t - d + 4) % 4
        passed.append(send(wf.at[o, mine], wp.at[o], partner))
    sent += first + passed

    rest = []
    for d in (1, 2, 3):
        q = (t + d) % 4
        for e in (1, 2, 3):
            block = wf.at[t, pl.ds(128 * ((q + e) % 4), 128)]
            rest.append(send(block, block, zpeer(0, d)))
    sent += rest

    for a in range(4):
        high, low = split(wf[a, mine])
        gh[a, 0:128] = high
        gl[a, 0:128] = low
    for copy in passed:
        copy.wait_recv()
    for a in range(4):
        high, low = split(wp[a])
        gh[a, 128:256] = high
        gl[a, 128:256] = low
    for k in range(5):
        (a0, b0), (a1, b1) = pairs[0][k], pairs[1][k]
        a, b = a0 + c * (a1 - a0), b0 + c * (b1 - b0)
        rows = ((0,), (0,))
        block = dot(gh[a], gh[b], rows) + (dot(gh[a], gl[b], rows) + dot(gl[a], gh[b], rows))
        part[0, 256 * k : 256 * k + 256] = block[:, :128]
        part[1, 256 * k : 256 * k + 256] = block[:, 128:]

    step = []
    for d in (1, 2, 3):
        step.append(send(part.at[0, pl.ds(320 * ((x + d) % 4), 320)], r1.at[0, d - 1], xpeer(d)))
        step.append(send(part.at[1, pl.ds(320 * ((y + d) % 4), 320)], r1.at[1, d - 1], ypeer(d)))
    for copy in step:
        copy.wait_recv()
    sent += step
    for h, i in ((0, x), (1, y)):
        own = part[h, pl.ds(pl.multiple_of(320 * i, 320), 320)]
        s1[h] = (own + r1[h, 0]) + (r1[h, 1] + r1[h, 2])

    step = []
    for d in (1, 2, 3):
        step.append(send(s1.at[0, pl.ds(80 * ((y + d) % 4), 80)], r2.at[0, d - 1], ypeer(d)))
        step.append(send(s1.at[1, pl.ds(80 * ((x + d) % 4), 80)], r2.at[1, d - 1], xpeer(d)))
    for copy in step:
        copy.wait_recv()
    sent += step
    for h, i in ((0, y), (1, x)):
        own = s1[h, pl.ds(pl.multiple_of(80 * i, 80), 80)]
        s2[80 * h : 80 * h + 80] = (own + r2[h, 0]) + (r2[h, 1] + r2[h, 2])

    step = []
    for dh in (0, 1):
        for d in range(4):
            if dh or d:
                step.append(send(s2.at[pl.ds(40 * ((t + d) % 4), 40)], r3.at[zh, t], zpeer(dh, d)))
    chunk = pl.ds(pl.multiple_of(40 * t, 40), 40)
    r3[zh, t] = s2[chunk]
    for copy in step:
        copy.wait_recv()
    sent += step
    total = r3[0, 0]
    for i in range(1, 8):
        total = total + r3[i // 4, i % 4]
    g2[chunk] = total

    step = []
    for d in (1, 2, 3):
        step.append(send(g2.at[chunk], g2.at[chunk], zpeer(0, d)))
    for copy in step:
        copy.wait_recv()
    sent += step
    step = []
    rows_y = pl.ds(pl.multiple_of(80 * y, 80), 80)
    rows_x = pl.ds(pl.multiple_of(80 * x, 80), 80)
    for d in (1, 2, 3):
        step.append(send(g2.at[pl.ds(0, 80)], g1.at[0, rows_y], ypeer(d)))
        step.append(send(g2.at[pl.ds(80, 80)], g1.at[1, rows_x], xpeer(d)))
    g1[0, rows_y] = g2[0:80]
    g1[1, rows_x] = g2[80:160]
    for copy in step:
        copy.wait_recv()
    sent += step
    step = []
    rows_x = pl.ds(pl.multiple_of(320 * x, 320), 320)
    rows_y = pl.ds(pl.multiple_of(320 * y, 320), 320)
    for d in (1, 2, 3):
        step.append(send(g1.at[0], gf.at[c, 0, rows_x], xpeer(d)))
        step.append(send(g1.at[1], gf.at[c, 1, rows_y], ypeer(d)))
    gf[c, 0, rows_x] = g1[0]
    gf[c, 1, rows_y] = g1[1]
    for copy in step:
        copy.wait_recv()
    sent += step
    swap = send(gf.at[c], gf.at[c], partner)
    sent.append(swap)
    swap.wait_recv()

    norm = jnp.zeros((1, 1), f32)
    for core in range(2):
        for k in range(5):
            a, b = pairs[core][k]
            block = jnp.concatenate(
                [gf[core, h, 256 * k : 256 * k + 256] for h in (0, 1)], axis=1
            )
            square = jnp.sum(jnp.sum(block * block, axis=0, keepdims=True), axis=1, keepdims=True)
            norm = norm + (square if a == b else 2.0 * square)
            high, low = split(block)
            gc[b, 256 * a : 256 * a + 256] = block
            gch[b, 256 * a : 256 * a + 256] = high
            gcl[b, 256 * a : 256 * a + 256] = low
            if a != b:
                block = block.T
                high, low = split(block)
                gc[a, 256 * b : 256 * b + 256] = block
                gch[a, 256 * b : 256 * b + 256] = high
                gcl[a, 256 * b : 256 * b + 256] = low
    factor = 2.0 / jnp.sqrt(norm + jnp.float32(1e-06))

    row = lax.broadcasted_iota(jnp.int32, (1024, 256), 0)
    col = lax.broadcasted_iota(jnp.int32, (1024, 256), 1)
    va[...] = jnp.where(row == col + 256 * t, 1.0, 0.0)
    vb[...] = factor * gc[t] - va[...]
    acc[...] = coefs[0] * va[...] + coefs[1] * vb[...]
    older, newer = va, vb
    for degree in (2, 3, 4):
        high, low = split(newer[...])
        vh[...] = high
        vl[...] = low
        for i in range(4):
            rows = slice(256 * i, 256 * i + 256)
            image = jnp.zeros((256, 256), f32)
            for k in range(4):
                kk = slice(256 * k, 256 * k + 256)
                image = image + (
                    dot(gch[k, rows], vh[kk])
                    + (dot(gch[k, rows], vl[kk]) + dot(gcl[k, rows], vh[kk]))
                )
            following = 2.0 * (factor * image - newer[rows]) - older[rows]
            acc[rows] = acc[rows] + coefs[degree] * following
            older[rows] = following
        older, newer = newer, older

    for copy in rest:
        copy.wait_recv()
    for a in range(4):
        high, low = split(wf[a])
        wfh[a] = high
        wfl[a] = low
    high, low = split(acc[...])
    vh[...] = high
    vl[...] = low
    for i in range(2):
        rows = slice(256 * i, 256 * i + 256)
        lowrank = jnp.zeros((256, 256), f32)
        for k in range(4):
            kk = slice(256 * k, 256 * k + 256)
            lowrank = lowrank + (
                dot(wfh[k, rows], vh[kk])
                + (dot(wfh[k, rows], vl[kk]) + dot(wfl[k, rows], vh[kk]))
            )
        level = tele[rows] - lowrank + mult[rows]
        size = jnp.maximum(jnp.abs(level) - shrink_level, 0.0)
        shrunk = jnp.where(level < 0.0, -size, size)
        low_out[rows] = lowrank
        sparse_out[rows] = shrunk
        mult_out[rows] = mult[rows] + tele[rows] - lowrank - shrunk
    for copy in sent:
        copy.wait_send()


copies = 3 + 4 + 9 + 6 + 6 + 7 + 3 + 6 + 6 + 1


def on_device(telemetry, sparse, multiplier):
    block = jax.ShapeDtypeStruct((512, 256), f32)
    vmem = pl.BlockSpec(memory_space=pltpu.VMEM)
    return pl.pallas_call(
        kernel,
        out_shape=(block, block, block),
        in_specs=[vmem] * 3,
        out_specs=(vmem, vmem, vmem),
        scratch_shapes=[
            pltpu.VMEM((4, 512, 256), f32),
            pltpu.VMEM((4, 128, 256), f32),
            pltpu.VMEM((4, 256, 256), bf16),
            pltpu.VMEM((4, 256, 256), bf16),
            pltpu.VMEM((2, 1280, 128), f32),
            pltpu.VMEM((2, 3, 320, 128), f32),
            pltpu.VMEM((2, 320, 128), f32),
            pltpu.VMEM((2, 3, 80, 128), f32),
            pltpu.VMEM((160, 128), f32),
            pltpu.VMEM((2, 4, 40, 128), f32),
            pltpu.VMEM((160, 128), f32),
            pltpu.VMEM((2, 320, 128), f32),
            pltpu.VMEM((2, 2, 1280, 128), f32),
            pltpu.VMEM((4, 1024, 256), f32),
            pltpu.VMEM((4, 1024, 256), bf16),
            pltpu.VMEM((4, 1024, 256), bf16),
            pltpu.VMEM((1024, 256), f32),
            pltpu.VMEM((1024, 256), f32),
            pltpu.VMEM((1024, 256), bf16),
            pltpu.VMEM((1024, 256), bf16),
            pltpu.VMEM((1024, 256), f32),
            pltpu.VMEM((4, 512, 256), bf16),
            pltpu.VMEM((4, 512, 256), bf16),
            pltpu.SemaphoreType.DMA((copies,)),
            pltpu.SemaphoreType.DMA((copies,)),
        ],
        compiler_params=pltpu.CompilerParams(
            collective_id=0, has_side_effects=True, vmem_limit_bytes=48 << 20
        ),
    )(telemetry, sparse, multiplier)


def solution(mesh):
    spec = P("series", "tick")
    return jax.shard_map(
        on_device,
        mesh=mesh,
        in_specs=(spec, spec, spec),
        out_specs=(spec, spec, spec),
        check_vma=False,
    )
```

```python
import functools

import jax
import jax.numpy as jnp
from jax import lax
from jax.experimental import pallas as pl
from jax.experimental.pallas import tpu as pltpu
from jax.sharding import PartitionSpec as P

MESH = pl.DeviceIdType.MESH
coefs = (0.4, 0.5, 0.1, -0.04, -0.06)
shrink_level = 0.5
f32, bf16 = jnp.float32, jnp.bfloat16

pairs = (
    ((0, 0), (0, 1), (0, 2), (0, 3), (1, 1)),
    ((1, 2), (1, 3), (2, 2), (2, 3), (3, 3)),
)


def split(value):
    high = value.astype(bf16)
    return high, (value - high.astype(f32)).astype(bf16)


def dot(a, b, dims=((1,), (0,))):
    return lax.dot_general(a, b, (dims, ((), ())), preferred_element_type=f32)


def kernel(
    tele_in, sparse_in, mult_in, low_out, sparse_out, mult_out,
    wf, wp, gh, gl, part, r1, s1, r2, s2, r3, g2, g1, gf,
    gc, gch, gcl, va, vb, vh, vl, acc, wfh, wfl, tele, sparse, mult, ls, ss, rs,
):
    series, t = lax.axis_index("series"), lax.axis_index("tick")
    c = series % 2
    x = (series // 2) % 4
    y = (series // 8) % 4
    zh = series // 32

    def at(zh_, t_, y_, x_, c_):
        return ((zh_ * 4 + y_) * 4 + x_) * 2 + c_, t_

    def xpeer(d):
        return at(zh, t, y, (x + d) % 4, c)

    def ypeer(d):
        return at(zh, t, (y + d) % 4, x, c)

    def zpeer(dh, d):
        return at((zh + dh) % 2, (t + d) % 4, y, x, c)

    partner = at(zh, t, y, x, 1 - c)
    count = [0]

    def send(src, dst, device):
        k = count[0]
        count[0] += 1
        copy = pltpu.make_async_remote_copy(
            src_ref=src, dst_ref=dst, send_sem=ss.at[k], recv_sem=rs.at[k],
            device_id=device, device_id_type=MESH,
        )
        copy.start()
        return copy

    sent = []
    rest = []

    loads = [
        pltpu.make_async_copy(src, dst, ls.at[i])
        for i, (src, dst) in enumerate(((tele_in, tele), (sparse_in, sparse), (mult_in, mult)))
    ]
    for load in loads:
        load.start()
    barrier = pltpu.get_barrier_semaphore()
    peers = [xpeer(d) for d in (1, 2, 3)] + [ypeer(d) for d in (1, 2, 3)]
    peers += [zpeer(dh, d) for dh in (0, 1) for d in range(4) if dh or d] + [partner]
    for p in peers:
        pl.semaphore_signal(barrier, inc=1, device_id=p, device_id_type=MESH)
    for load in loads:
        load.wait()
    wf[t] = tele[...] - sparse[...] + mult[...]
    pl.semaphore_wait(barrier, len(peers))

    first = []
    for d in (1, 2, 3):
        q = (t + d) % 4
        block = wf.at[t, pl.ds(128 * q, 128)]
        first.append(send(block, block, zpeer(0, d)))
    mine = pl.ds(pl.multiple_of(128 * t, 128), 128)
    passed = [send(wf.at[t, mine], wp.at[t], partner)]
    for d in (1, 2, 3):
        first[d - 1].wait_recv()
        o = (t - d + 4) % 4
        passed.append(send(wf.at[o, mine], wp.at[o], partner))
    sent += first + passed

    def spread(kinds):
        for d, e in kinds:
            q = (t + d) % 4
            block = wf.at[t, pl.ds(128 * ((q + e) % 4), 128)]
            rest.append(send(block, block, zpeer(0, d)))

    for a in range(4):
        high, low = split(wf[a, mine])
        gh[a, 0:128] = high
        gl[a, 0:128] = low
    for copy in passed:
        copy.wait_recv()
    for a in range(4):
        high, low = split(wp[a])
        gh[a, 128:256] = high
        gl[a, 128:256] = low
    for k in range(5):
        (a0, b0), (a1, b1) = pairs[0][k], pairs[1][k]
        a, b = a0 + c * (a1 - a0), b0 + c * (b1 - b0)
        rows = ((0,), (0,))
        block = dot(gh[a], gh[b], rows) + (dot(gh[a], gl[b], rows) + dot(gl[a], gh[b], rows))
        part[0, 256 * k : 256 * k + 256] = block[:, :128]
        part[1, 256 * k : 256 * k + 256] = block[:, 128:]

    spread(((2, 1), (1, 1), (3, 1), (1, 2), (3, 2)))
    step = []
    for d in (1, 2, 3):
        step.append(send(part.at[0, pl.ds(320 * ((x + d) % 4), 320)], r1.at[0, d - 1], xpeer(d)))
        step.append(send(part.at[1, pl.ds(320 * ((y + d) % 4), 320)], r1.at[1, d - 1], ypeer(d)))
    for copy in step:
        copy.wait_recv()
    sent += step
    for h, i in ((0, x), (1, y)):
        own = part[h, pl.ds(pl.multiple_of(320 * i, 320), 320)]
        s1[h] = (own + r1[h, 0]) + (r1[h, 1] + r1[h, 2])

    step = []
    for d in (1, 2, 3):
        step.append(send(s1.at[0, pl.ds(80 * ((y + d) % 4), 80)], r2.at[0, d - 1], ypeer(d)))
        step.append(send(s1.at[1, pl.ds(80 * ((x + d) % 4), 80)], r2.at[1, d - 1], xpeer(d)))
    for copy in step:
        copy.wait_recv()
    sent += step
    for h, i in ((0, y), (1, x)):
        own = s1[h, pl.ds(pl.multiple_of(80 * i, 80), 80)]
        s2[80 * h : 80 * h + 80] = (own + r2[h, 0]) + (r2[h, 1] + r2[h, 2])

    step = []
    for dh in (0, 1):
        for d in range(4):
            if dh or d:
                step.append(send(s2.at[pl.ds(40 * ((t + d) % 4), 40)], r3.at[zh, t], zpeer(dh, d)))
    chunk = pl.ds(pl.multiple_of(40 * t, 40), 40)
    r3[zh, t] = s2[chunk]
    for copy in step:
        copy.wait_recv()
    sent += step
    total = r3[0, 0]
    for i in range(1, 8):
        total = total + r3[i // 4, i % 4]
    g2[chunk] = total

    step = []
    for d in (1, 2, 3):
        step.append(send(g2.at[chunk], g2.at[chunk], zpeer(0, d)))
    for copy in step:
        copy.wait_recv()
    sent += step
    spread(((2, 2), (2, 3), (1, 3), (3, 3)))
    step = []
    rows_y = pl.ds(pl.multiple_of(80 * y, 80), 80)
    rows_x = pl.ds(pl.multiple_of(80 * x, 80), 80)
    for d in (1, 2, 3):
        step.append(send(g2.at[pl.ds(0, 80)], g1.at[0, rows_y], ypeer(d)))
        step.append(send(g2.at[pl.ds(80, 80)], g1.at[1, rows_x], xpeer(d)))
    g1[0, rows_y] = g2[0:80]
    g1[1, rows_x] = g2[80:160]
    for copy in step:
        copy.wait_recv()
    sent += step
    step = []
    rows_x = pl.ds(pl.multiple_of(320 * x, 320), 320)
    rows_y = pl.ds(pl.multiple_of(320 * y, 320), 320)
    for d in (1, 2, 3):
        step.append(send(g1.at[0], gf.at[c, 0, rows_x], xpeer(d)))
        step.append(send(g1.at[1], gf.at[c, 1, rows_y], ypeer(d)))
    gf[c, 0, rows_x] = g1[0]
    gf[c, 1, rows_y] = g1[1]
    swap = []
    for h, i in ((0, x), (1, y)):
        piece = gf.at[c, h, pl.ds(320 * i, 320)]
        swap.append(send(piece, piece, partner))
    for d in (1, 2, 3):
        for h, i in ((0, x), (1, y)):
            step[2 * (d - 1) + h].wait_recv()
            piece = gf.at[c, h, pl.ds(320 * ((i - d + 4) % 4), 320)]
            swap.append(send(piece, piece, partner))
    for copy in swap:
        copy.wait_recv()
    sent += step + swap
    norm = jnp.zeros((1, 1), f32)
    for core in range(2):
        for k in range(5):
            a, b = pairs[core][k]
            block = jnp.concatenate(
                [gf[core, h, 256 * k : 256 * k + 256] for h in (0, 1)], axis=1
            )
            square = jnp.sum(jnp.sum(block * block, axis=0, keepdims=True), axis=1, keepdims=True)
            norm = norm + (square if a == b else 2.0 * square)
            high, low = split(block)
            gc[b, 256 * a : 256 * a + 256] = block
            gch[b, 256 * a : 256 * a + 256] = high
            gcl[b, 256 * a : 256 * a + 256] = low
            if a != b:
                block = block.T
                high, low = split(block)
                gc[a, 256 * b : 256 * b + 256] = block
                gch[a, 256 * b : 256 * b + 256] = high
                gcl[a, 256 * b : 256 * b + 256] = low
    factor = 2.0 / jnp.sqrt(norm + jnp.float32(1e-06))

    row = lax.broadcasted_iota(jnp.int32, (1024, 256), 0)
    col = lax.broadcasted_iota(jnp.int32, (1024, 256), 1)
    va[...] = jnp.where(row == col + 256 * t, 1.0, 0.0)
    vb[...] = factor * gc[t] - va[...]
    acc[...] = coefs[0] * va[...] + coefs[1] * vb[...]
    older, newer = va, vb
    for degree in (2, 3, 4):
        high, low = split(newer[...])
        vh[...] = high
        vl[...] = low
        for i in range(4):
            rows = slice(256 * i, 256 * i + 256)
            image = jnp.zeros((256, 256), f32)
            for k in range(4):
                kk = slice(256 * k, 256 * k + 256)
                image = image + (
                    dot(gch[k, rows], vh[kk])
                    + (dot(gch[k, rows], vl[kk]) + dot(gcl[k, rows], vh[kk]))
                )
            following = 2.0 * (factor * image - newer[rows]) - older[rows]
            acc[rows] = acc[rows] + coefs[degree] * following
            older[rows] = following
        older, newer = newer, older

    for copy in rest:
        copy.wait_recv()
    for a in range(4):
        high, low = split(wf[a])
        wfh[a] = high
        wfl[a] = low
    high, low = split(acc[...])
    vh[...] = high
    vl[...] = low
    for i in range(2):
        rows = slice(256 * i, 256 * i + 256)
        lowrank = jnp.zeros((256, 256), f32)
        for k in range(4):
            kk = slice(256 * k, 256 * k + 256)
            lowrank = lowrank + (
                dot(wfh[k, rows], vh[kk])
                + (dot(wfh[k, rows], vl[kk]) + dot(wfl[k, rows], vh[kk]))
            )
        level = tele[rows] - lowrank + mult[rows]
        size = jnp.maximum(jnp.abs(level) - shrink_level, 0.0)
        shrunk = jnp.where(level < 0.0, -size, size)
        low_out[rows] = lowrank
        sparse_out[rows] = shrunk
        mult_out[rows] = mult[rows] + tele[rows] - lowrank - shrunk
    for copy in sent + rest:
        copy.wait_send()


copies = 3 + 4 + 9 + 6 + 6 + 7 + 3 + 6 + 6 + 8


def on_device(telemetry, sparse, multiplier):
    block = jax.ShapeDtypeStruct((512, 256), f32)
    vmem = pl.BlockSpec(memory_space=pltpu.VMEM)
    return pl.pallas_call(
        kernel,
        out_shape=(block, block, block),
        in_specs=[pl.BlockSpec(memory_space=pltpu.HBM)] * 3,
        out_specs=(vmem, vmem, vmem),
        scratch_shapes=[
            pltpu.VMEM((4, 512, 256), f32),
            pltpu.VMEM((4, 128, 256), f32),
            pltpu.VMEM((4, 256, 256), bf16),
            pltpu.VMEM((4, 256, 256), bf16),
            pltpu.VMEM((2, 1280, 128), f32),
            pltpu.VMEM((2, 3, 320, 128), f32),
            pltpu.VMEM((2, 320, 128), f32),
            pltpu.VMEM((2, 3, 80, 128), f32),
            pltpu.VMEM((160, 128), f32),
            pltpu.VMEM((2, 4, 40, 128), f32),
            pltpu.VMEM((160, 128), f32),
            pltpu.VMEM((2, 320, 128), f32),
            pltpu.VMEM((2, 2, 1280, 128), f32),
            pltpu.VMEM((4, 1024, 256), f32),
            pltpu.VMEM((4, 1024, 256), bf16),
            pltpu.VMEM((4, 1024, 256), bf16),
            pltpu.VMEM((1024, 256), f32),
            pltpu.VMEM((1024, 256), f32),
            pltpu.VMEM((1024, 256), bf16),
            pltpu.VMEM((1024, 256), bf16),
            pltpu.VMEM((1024, 256), f32),
            pltpu.VMEM((4, 512, 256), bf16),
            pltpu.VMEM((4, 512, 256), bf16),
            pltpu.VMEM((512, 256), f32),
            pltpu.VMEM((512, 256), f32),
            pltpu.VMEM((512, 256), f32),
            pltpu.SemaphoreType.DMA((3,)),
            pltpu.SemaphoreType.DMA((copies,)),
            pltpu.SemaphoreType.DMA((copies,)),
        ],
        compiler_params=pltpu.CompilerParams(
            collective_id=0, has_side_effects=True, vmem_limit_bytes=56 << 20
        ),
    )(telemetry, sparse, multiplier)


def solution(mesh):
    spec = P("series", "tick")
    return jax.shard_map(
        on_device,
        mesh=mesh,
        in_specs=(spec, spec, spec),
        out_specs=(spec, spec, spec),
        check_vma=False,
    )
```

```python
import functools

import jax
import jax.numpy as jnp
from jax import lax
from jax.experimental import pallas as pl
from jax.experimental.pallas import tpu as pltpu
from jax.sharding import PartitionSpec as P

MESH = pl.DeviceIdType.MESH
coefs = (0.4, 0.5, 0.1, -0.04, -0.06)
shrink_level = 0.5
f32, bf16 = jnp.float32, jnp.bfloat16

pairs = (
    ((0, 0), (0, 1), (0, 2), (0, 3), (1, 1)),
    ((1, 2), (1, 3), (2, 2), (2, 3), (3, 3)),
)


def split(value):
    high = value.astype(bf16)
    return high, (value - high.astype(f32)).astype(bf16)


def dot(a, b, dims=((1,), (0,))):
    return lax.dot_general(a, b, (dims, ((), ())), preferred_element_type=f32)


def kernel(
    tele_in, sparse_in, mult_in, low_out,
    wf, wp, gh, gl, part, r1, s1, r2, s2, r3, g2, gf,
    gc, gch, gcl, va, vb, vh, vl, acc, wfh, wfl, tele, sparse, mult, ls, ss, rs,
):
    series, t = lax.axis_index("series"), lax.axis_index("tick")
    c = series % 2
    x = (series // 2) % 4
    y = (series // 8) % 4
    zh = series // 32

    def at(zh_, t_, y_, x_, c_):
        return ((zh_ * 4 + y_) * 4 + x_) * 2 + c_, t_

    def xpeer(d):
        return at(zh, t, y, (x + d) % 4, c)

    def ypeer(d):
        return at(zh, t, (y + d) % 4, x, c)

    def zpeer(dh, d):
        return at((zh + dh) % 2, (t + d) % 4, y, x, c)

    partner = at(zh, t, y, x, 1 - c)
    count = [0]

    def send(src, dst, device, here=None):
        k = count[0]
        count[0] += 1
        copy = pltpu.make_async_remote_copy(
            src_ref=src, dst_ref=dst, send_sem=ss.at[k], recv_sem=rs.at[k],
            device_id=device, device_id_type=MESH,
        )
        if here is None:
            copy.start()
        else:
            pl.when(here)(copy.start)
        return copy

    sent = []
    rest = []

    loads = [
        pltpu.make_async_copy(src, dst, ls.at[i])
        for i, (src, dst) in enumerate(((tele_in, tele), (sparse_in, sparse), (mult_in, mult)))
    ]
    for load in loads:
        load.start()
    barrier = pltpu.get_barrier_semaphore()
    peers = [xpeer(d) for d in (1, 2, 3)] + [ypeer(d) for d in (1, 2, 3)]
    peers += [zpeer(dh, d) for dh in (0, 1) for d in range(4) if dh or d] + [partner]
    for p in peers:
        pl.semaphore_signal(barrier, inc=1, device_id=p, device_id_type=MESH)
    for load in loads:
        load.wait()
    wf[t] = tele[...] - sparse[...] + mult[...]
    pl.semaphore_wait(barrier, len(peers))

    first = []
    for d in (1, 2, 3):
        q = (t + d) % 4
        block = wf.at[t, pl.ds(128 * q, 128)]
        first.append(send(block, block, zpeer(0, d)))
    mine = pl.ds(pl.multiple_of(128 * t, 128), 128)
    passed = [send(wf.at[t, mine], wp.at[t], partner)]
    for d in (1, 2, 3):
        first[d - 1].wait_recv()
        o = (t - d + 4) % 4
        passed.append(send(wf.at[o, mine], wp.at[o], partner))
    sent += first + passed

    middle = (t - 1) * (t - 2) == 0
    side = 1 - t // 2

    def spread(d, e):
        q = (t + d) % 4
        block = wf.at[t, pl.ds(128 * ((q + e) % 4), 128)]
        here, there = {1: (t != 3, t != 0), 2: (None, None), 3: (t != 0, t != 3)}[d]
        rest.append((send(block, block, zpeer(0, d), here), here, there))

    def relay(r):
        block = wf.at[3 * side, pl.ds(128 * r, 128)]
        rest.append((send(block, block, at(zh, 3 * (t // 2), y, x, c), middle), middle, (t - 1) * (t - 2) != 0))

    for a in range(4):
        high, low = split(wf[a, mine])
        gh[a, 0:128] = high
        gl[a, 0:128] = low
    for copy in passed:
        copy.wait_recv()
    for a in range(4):
        high, low = split(wp[a])
        gh[a, 128:256] = high
        gl[a, 128:256] = low
    for k in range(5):
        (a0, b0), (a1, b1) = pairs[0][k], pairs[1][k]
        a, b = a0 + c * (a1 - a0), b0 + c * (b1 - b0)
        rows = ((0,), (0,))
        block = dot(gh[a], gh[b], rows) + (dot(gh[a], gl[b], rows) + dot(gl[a], gh[b], rows))
        part[0, 256 * k : 256 * k + 256] = block[:, :128]
        part[1, 256 * k : 256 * k + 256] = block[:, 128:]

    for k in (0, 1):
        spread(2, (k + side) % 3 + 1)
    relay(t)
    spread(1, 1)
    spread(3, 1)
    def first_at(h, i, n):
        return pl.ds(pl.multiple_of(320 * i + 80 * ((((y, x)[h]) + n) % 4), 80), 80)

    order = (2, 1, 3)
    step = {}
    for n in order + (0,):
        for d in order:
            for h in (0, 1):
                i, peer = ((x, xpeer), (y, ypeer))[h]
                step[n, d, h] = send(part.at[h, first_at(h, (i + d) % 4, n)], r1.at[h, d - 1, n], peer(d))
    step2 = {}
    for n in order + (0,):
        for h in (0, 1):
            i, peer = ((x, ypeer), (y, xpeer))[h]
            for d in order:
                step[n, d, h].wait_recv()
            value = (part[h, first_at(h, i, n)] + r1[h, 0, n]) + (r1[h, 1, n] + r1[h, 2, n])
            if n:
                s1[h, n - 1] = value
                step2[n, h] = send(s1.at[h, n - 1], r2.at[h, n - 1], peer(n))
            else:
                s2[80 * h : 80 * h + 80] = value
    sent += list(step.values()) + list(step2.values())
    for h in (0, 1):
        for n in order:
            step2[n, h].wait_recv()
        rows = slice(80 * h, 80 * h + 80)
        s2[rows] = (s2[rows] + r2[h, 0]) + (r2[h, 1] + r2[h, 2])

    step = []
    for dh in (1, 0):
        for d in (0, 2, 1, 3):
            if dh or d:
                step.append(send(s2.at[pl.ds(40 * ((t + d) % 4), 40)], r3.at[zh, t], zpeer(dh, d)))
    chunk = pl.ds(pl.multiple_of(40 * t, 40), 40)
    r3[zh, t] = s2[chunk]
    for copy in step:
        copy.wait_recv()
    sent += step
    total = r3[0, 0]
    for i in range(1, 8):
        total = total + r3[i // 4, i % 4]
    g2[chunk] = total

    step = []
    for d in (1, 2, 3):
        step.append(send(g2.at[chunk], g2.at[chunk], zpeer(0, d)))
    for copy in step:
        copy.wait_recv()
    sent += step
    for k in (0, 1):
        rest[k][0].wait_recv()
        relay((2 * side + k) % 4)
    spread(2, (2 + side) % 3 + 1)
    for e in (2, 3):
        spread(1, e)
        spread(3, e)
    def last_at(h, d, n):
        own = (320 * ((x - d + 4) % 4) + 80 * ((y - n + 4) % 4), 320 * ((y - d + 4) % 4) + 80 * ((x - n + 4) % 4))[h]
        return pl.ds(pl.multiple_of(own, 80), 80)

    gathered, swap = {}, []

    def onward(h, n):
        piece = gf.at[c, h, last_at(h, 0, n)]
        for d in order:
            gathered[n, d, h] = send(piece, piece, (xpeer, ypeer)[h](d))
        swap.append(send(piece, piece, partner))

    for h in (0, 1):
        gf[c, h, last_at(h, 0, 0)] = g2[80 * h : 80 * h + 80]
    step = {}
    for d in order:
        for h in (0, 1):
            piece = gf.at[c, h, last_at(h, 0, 0)]
            step[d, h] = send(piece, piece, (ypeer, xpeer)[h](d))
    for h in (0, 1):
        onward(h, 0)
    for n in (1, 3, 2):
        for h in (0, 1):
            step[n, h].wait_recv()
            onward(h, n)
    for n in (0, 1, 3, 2):
        for d in (1, 3, 2):
            for h in (0, 1):
                gathered[n, d, h].wait_recv()
                piece = gf.at[c, h, last_at(h, d, n)]
                swap.append(send(piece, piece, partner))
    for copy in swap:
        copy.wait_recv()
    sent += list(step.values()) + list(gathered.values()) + swap
    norm = jnp.zeros((1, 1), f32)
    for core in range(2):
        for k in range(5):
            a, b = pairs[core][k]
            block = jnp.concatenate(
                [gf[core, h, 256 * k : 256 * k + 256] for h in (0, 1)], axis=1
            )
            square = jnp.sum(jnp.sum(block * block, axis=0, keepdims=True), axis=1, keepdims=True)
            norm = norm + (square if a == b else 2.0 * square)
            high, low = split(block)
            gc[b, 256 * a : 256 * a + 256] = block
            gch[b, 256 * a : 256 * a + 256] = high
            gcl[b, 256 * a : 256 * a + 256] = low
            if a != b:
                block = block.T
                high, low = split(block)
                gc[a, 256 * b : 256 * b + 256] = block
                gch[a, 256 * b : 256 * b + 256] = high
                gcl[a, 256 * b : 256 * b + 256] = low
    factor = 2.0 / jnp.sqrt(norm + jnp.float32(1e-06))

    row = lax.broadcasted_iota(jnp.int32, (1024, 256), 0)
    col = lax.broadcasted_iota(jnp.int32, (1024, 256), 1)
    va[...] = jnp.where(row == col + 256 * t, 1.0, 0.0)
    vb[...] = factor * gc[t] - va[...]
    acc[...] = coefs[0] * va[...] + coefs[1] * vb[...]
    older, newer = va, vb
    for degree in (2, 3, 4):
        high, low = split(newer[...])
        vh[...] = high
        vl[...] = low
        for i in range(4):
            rows = slice(256 * i, 256 * i + 256)
            image = jnp.zeros((256, 256), f32)
            for k in range(4):
                kk = slice(256 * k, 256 * k + 256)
                image = image + (
                    dot(gch[k, rows], vh[kk])
                    + (dot(gch[k, rows], vl[kk]) + dot(gcl[k, rows], vh[kk]))
                )
            following = 2.0 * (factor * image - newer[rows]) - older[rows]
            acc[rows] = acc[rows] + coefs[degree] * following
            older[rows] = following
        older, newer = newer, older

    for copy, _, there in rest[2:]:
        if there is None:
            copy.wait_recv()
        else:
            pl.when(there)(copy.wait_recv)
    for a in range(4):
        high, low = split(wf[a])
        wfh[a] = high
        wfl[a] = low
    high, low = split(acc[...])
    vh[...] = high
    vl[...] = low
    for i in range(2):
        rows = slice(256 * i, 256 * i + 256)
        lowrank = jnp.zeros((256, 256), f32)
        for k in range(4):
            kk = slice(256 * k, 256 * k + 256)
            lowrank = lowrank + (
                dot(wfh[k, rows], vh[kk])
                + (dot(wfh[k, rows], vl[kk]) + dot(wfl[k, rows], vh[kk]))
            )
        low_out[rows] = 0.5 * lowrank
    for copy in sent:
        copy.wait_send()
    for copy, here, _ in rest:
        if here is None:
            copy.wait_send()
        else:
            pl.when(here)(copy.wait_send)


copies = 3 + 4 + 12 + 24 + 6 + 7 + 3 + 6 + 24 + 32


def on_device(telemetry, sparse, multiplier):
    block = jax.ShapeDtypeStruct((512, 256), f32)
    vmem = pl.BlockSpec(memory_space=pltpu.VMEM)
    half = pl.pallas_call(
        kernel,
        out_shape=block,
        in_specs=[pl.BlockSpec(memory_space=pltpu.HBM)] * 3,
        out_specs=vmem,
        scratch_shapes=[
            pltpu.VMEM((4, 512, 256), f32),
            pltpu.VMEM((4, 128, 256), f32),
            pltpu.VMEM((4, 256, 256), bf16),
            pltpu.VMEM((4, 256, 256), bf16),
            pltpu.VMEM((2, 1280, 128), f32),
            pltpu.VMEM((2, 3, 4, 80, 128), f32),
            pltpu.VMEM((2, 3, 80, 128), f32),
            pltpu.VMEM((2, 3, 80, 128), f32),
            pltpu.VMEM((160, 128), f32),
            pltpu.VMEM((2, 4, 40, 128), f32),
            pltpu.VMEM((160, 128), f32),
            pltpu.VMEM((2, 2, 1280, 128), f32),
            pltpu.VMEM((4, 1024, 256), f32),
            pltpu.VMEM((4, 1024, 256), bf16),
            pltpu.VMEM((4, 1024, 256), bf16),
            pltpu.VMEM((1024, 256), f32),
            pltpu.VMEM((1024, 256), f32),
            pltpu.VMEM((1024, 256), bf16),
            pltpu.VMEM((1024, 256), bf16),
            pltpu.VMEM((1024, 256), f32),
            pltpu.VMEM((4, 512, 256), bf16),
            pltpu.VMEM((4, 512, 256), bf16),
            pltpu.VMEM((512, 256), f32),
            pltpu.VMEM((512, 256), f32),
            pltpu.VMEM((512, 256), f32),
            pltpu.SemaphoreType.DMA((3,)),
            pltpu.SemaphoreType.DMA((copies,)),
            pltpu.SemaphoreType.DMA((copies,)),
        ],
        compiler_params=pltpu.CompilerParams(
            collective_id=0, has_side_effects=True, vmem_limit_bytes=56 << 20
        ),
    )(telemetry, sparse, multiplier)
    lowrank = 2.0 * half
    level = telemetry - lowrank + multiplier
    size = jnp.maximum(jnp.abs(level) - shrink_level, 0.0)
    new_sparse = jnp.where(level < 0.0, -size, size)
    return lowrank, new_sparse, multiplier + telemetry - lowrank - new_sparse


def solution(mesh):
    spec = P("series", "tick")
    return jax.shard_map(
        on_device,
        mesh=mesh,
        in_specs=(spec, spec, spec),
        out_specs=(spec, spec, spec),
        check_vma=False,
    )
```

```python
import functools

import jax
import jax.numpy as jnp
from jax import lax
from jax.experimental import pallas as pl
from jax.experimental.pallas import tpu as pltpu
from jax.sharding import PartitionSpec as P

MESH = pl.DeviceIdType.MESH
coefs = (0.4, 0.5, 0.1, -0.04, -0.06)
shrink_level = 0.5
f32, bf16 = jnp.float32, jnp.bfloat16

pairs = (((0, 1), (0, 2), (0, 3)), ((1, 2), (1, 3), (2, 3)))


def split(value):
    high = value.astype(bf16)
    return high, (value - high.astype(f32)).astype(bf16)


def dot(a, b, dims=((1,), (0,))):
    return lax.dot_general(a, b, (dims, ((), ())), preferred_element_type=f32)


def kernel(
    tele_in, sparse_in, mult_in, low_out,
    wf, wp, dh, dl, dpart, dother, dr1, ds1, dr2, ds2, drz, gd, gh, gl, part, r1, s1, r2, s2, r3, g2, gf,
    gc, gch, gcl, va, vb, vh, vl, acc, wfh, wfl, tele, sparse, mult, ls, ss, rs,
):
    series, t = lax.axis_index("series"), lax.axis_index("tick")
    c = series % 2
    x = (series // 2) % 4
    y = (series // 8) % 4
    zh = series // 32

    def at(zh_, t_, y_, x_, c_):
        return ((zh_ * 4 + y_) * 4 + x_) * 2 + c_, t_

    def xpeer(d):
        return at(zh, t, y, (x + d) % 4, c)

    def ypeer(d):
        return at(zh, t, (y + d) % 4, x, c)

    def zpeer(dh, d):
        return at((zh + dh) % 2, (t + d) % 4, y, x, c)

    partner = at(zh, t, y, x, 1 - c)
    count = [0]

    def send(src, dst, device, here=None):
        k = count[0]
        count[0] += 1
        copy = pltpu.make_async_remote_copy(
            src_ref=src, dst_ref=dst, send_sem=ss.at[k], recv_sem=rs.at[k],
            device_id=device, device_id_type=MESH,
        )
        if here is None:
            copy.start()
        else:
            pl.when(here)(copy.start)
        return copy

    sent = []

    loads = [
        pltpu.make_async_copy(src, dst, ls.at[i])
        for i, (src, dst) in enumerate(((tele_in, tele), (sparse_in, sparse), (mult_in, mult)))
    ]
    for load in loads:
        load.start()
    barrier = pltpu.get_barrier_semaphore()
    peers = [xpeer(d) for d in (1, 2, 3)] + [ypeer(d) for d in (1, 2, 3)]
    peers += [zpeer(dh, d) for dh in (0, 1) for d in range(4) if dh or d] + [partner]
    for p in peers:
        pl.semaphore_signal(barrier, inc=1, device_id=p, device_id_type=MESH)
    for load in loads:
        load.wait()
    wf[t] = tele[...] - sparse[...] + mult[...]
    pl.semaphore_wait(barrier, len(peers))

    first = []
    for d in (1, 2, 3):
        q = (t + d) % 4
        block = wf.at[t, pl.ds(128 * q, 128)]
        first.append(send(block, block, zpeer(0, d)))
    middle = (t - 1) * (t - 2) == 0
    ends = (t - 1) * (t - 2) != 0
    side = 1 - t // 2
    rest = []

    def spread(d, e, early=None):
        q = (t + d) % 4
        block = wf.at[t, pl.ds(128 * ((q + e) % 4), 128)]
        here, there = {1: (t != 3, t != 0), 2: (ends, middle), 3: (t != 0, t != 3)}[d]
        copy = send(block, block, zpeer(0, d), here if early is None else early)
        rest.append((copy, here, there))
        return copy

    def relay(o, r):
        block = wf.at[o, pl.ds(128 * r, 128)]
        rest.append((send(block, block, at(zh, 3 * (t // 2), y, x, c), middle), middle, ends))

    near = [spread(1, 2, t % 2 == 0), spread(3, 1, t % 2 == 1)]
    mine = pl.ds(pl.multiple_of(128 * t, 128), 128)
    passed = [send(wf.at[t, mine], wp.at[t], partner)]

    order = (2, 1, 3)
    cols = ((0,), (0,))
    high, low = split(wf[t])
    dh[...] = high
    dl[...] = low
    block = dot(dh[...], dh[...], cols) + (dot(dh[...], dl[...], cols) + dot(dl[...], dh[...], cols))
    for h in (0, 1):
        dpart[h] = block[:, 128 * h : 128 * h + 128]
    low_half = pl.ds(pl.multiple_of(128 * c, 128), 128)
    high_half = pl.ds(pl.multiple_of(128 * (1 - c), 128), 128)
    cross = send(dpart.at[:, high_half], dother, partner)
    cross.wait_recv()
    for h in (0, 1):
        dother[h] = dpart[h, low_half] + dother[h]
    step = {}
    for d in order:
        step[d, 0] = send(dother.at[0, pl.ds(32 * ((x + d) % 4), 32)], dr1.at[0, d - 1], xpeer(d))
        step[d, 1] = send(dother.at[1, pl.ds(32 * ((y + d) % 4), 32)], dr1.at[1, d - 1], ypeer(d))
    step2 = {}
    for h, i in ((0, x), (1, y)):
        for d in order:
            step[d, h].wait_recv()
        own = dother[h, pl.ds(pl.multiple_of(32 * i, 32), 32)]
        ds1[h] = (own + dr1[h, 0]) + (dr1[h, 1] + dr1[h, 2])
        i, peer = ((y, ypeer), (x, xpeer))[h]
        for d in order:
            step2[d, h] = send(ds1.at[h, pl.ds(8 * ((i + d) % 4), 8)], dr2.at[h, d - 1], peer(d))
    sent += [cross] + list(step.values()) + list(step2.values())

    for d in (1, 2, 3):
        first[d - 1].wait_recv()
        o = (t - d + 4) % 4
        passed.append(send(wf.at[o, mine], wp.at[o], partner))
    sent += first + passed
    for h, i in ((0, y), (1, x)):
        for d in order:
            step2[d, h].wait_recv()
        own = ds1[h, pl.ds(pl.multiple_of(8 * i, 8), 8)]
        ds2[h] = (own + dr2[h, 0]) + (dr2[h, 1] + dr2[h, 2])

    along = []
    for flip in (1, 0):
        for d in (0, 2, 1, 3):
            if flip or d:
                along.append(send(ds2, drz.at[zh, t], zpeer(flip, d)))
    drz[zh, t] = ds2[...]
    sent += along
    pl.when(t == 1)(near[0].start)
    pl.when(t == 2)(near[1].start)
    relay(3 * side, t)
    relay((3 - t) % 4, t)
    for k in (0, 1):
        spread(2, (k + side) % 3 + 1)
    spread(1, 3)
    spread(3, 2)

    for a in range(4):
        high, low = split(wf[a, mine])
        gh[a, 0:128] = high
        gl[a, 0:128] = low
    for copy in passed:
        copy.wait_recv()
    for a in range(4):
        high, low = split(wp[a])
        gh[a, 128:256] = high
        gl[a, 128:256] = low
    for k in range(3):
        (a0, b0), (a1, b1) = pairs[0][k], pairs[1][k]
        a, b = a0 + c * (a1 - a0), b0 + c * (b1 - b0)
        rows = ((0,), (0,))
        block = dot(gh[a], gh[b], rows) + (dot(gh[a], gl[b], rows) + dot(gl[a], gh[b], rows))
        part[0, 256 * k : 256 * k + 256] = block[:, :128]
        part[1, 256 * k : 256 * k + 256] = block[:, 128:]

    def first_at(h, i, n):
        return pl.ds(pl.multiple_of(192 * i + 48 * ((((y, x)[h]) + n) % 4), 48), 48)

    step = {}
    for n in order + (0,):
        for d in order:
            for h in (0, 1):
                i, peer = ((x, xpeer), (y, ypeer))[h]
                step[n, d, h] = send(part.at[h, first_at(h, (i + d) % 4, n)], r1.at[h, d - 1, n], peer(d))
    step2 = {}
    for n in order + (0,):
        for h in (0, 1):
            i, peer = ((x, ypeer), (y, xpeer))[h]
            for d in order:
                step[n, d, h].wait_recv()
            value = (part[h, first_at(h, i, n)] + r1[h, 0, n]) + (r1[h, 1, n] + r1[h, 2, n])
            if n:
                s1[h, n - 1] = value
                step2[n, h] = send(s1.at[h, n - 1], r2.at[h, n - 1], peer(n))
            else:
                s2[48 * h : 48 * h + 48] = value
    sent += list(step.values()) + list(step2.values())
    for copy in along:
        copy.wait_recv()
    back = []
    for h, i, peer in ((0, 4 * x + y, ypeer), (1, 4 * y + x, xpeer)):
        for tick in range(4):
            gd[c, h, i, tick] = drz[0, tick, h] + drz[1, tick, h]
        for d in order:
            back.append(send(gd.at[c, h, i], gd.at[c, h, i], peer(d)))
    sent += back
    for h in (0, 1):
        for n in order:
            step2[n, h].wait_recv()
        rows = slice(48 * h, 48 * h + 48)
        s2[rows] = (s2[rows] + r2[h, 0]) + (r2[h, 1] + r2[h, 2])

    step = []
    for dh in (1, 0):
        for d in (0, 2, 1, 3):
            if dh or d:
                step.append(send(s2.at[pl.ds(24 * ((t + d) % 4), 24)], r3.at[zh, t], zpeer(dh, d)))
    chunk = pl.ds(pl.multiple_of(24 * t, 24), 24)
    r3[zh, t] = s2[chunk]
    for copy in back:
        copy.wait_recv()
    back = []
    for h, i, peer in ((0, x, xpeer), (1, y, ypeer)):
        row = gd.at[c, h, pl.ds(4 * i, 4)]
        for d in order:
            back.append(send(row, row, peer(d)))
    sent += back
    for copy in step:
        copy.wait_recv()
    sent += step
    total = r3[0, 0]
    for i in range(1, 8):
        total = total + r3[i // 4, i % 4]
    g2[chunk] = total

    step = []
    for d in (1, 2, 3):
        step.append(send(g2.at[chunk], g2.at[chunk], zpeer(0, d)))
    for copy in step:
        copy.wait_recv()
    sent += step
    early = len(rest)
    for copy, _, there in rest:
        pl.when(there)(copy.wait_recv)
    for k in (0, 1):
        relay(3 * side, 2 * side + k)
        relay((3 - t) % 4, 2 * side + k)
    spread(2, (2 + side) % 3 + 1)
    spread(1, 1)
    spread(3, 3)
    def last_at(h, d, n):
        own = (192 * ((x - d + 4) % 4) + 48 * ((y - n + 4) % 4), 192 * ((y - d + 4) % 4) + 48 * ((x - n + 4) % 4))[h]
        return pl.ds(pl.multiple_of(own, 48), 48)

    gathered, swap = {}, []

    def onward(h, n):
        piece = gf.at[c, h, last_at(h, 0, n)]
        for d in order:
            gathered[n, d, h] = send(piece, piece, (xpeer, ypeer)[h](d))
        swap.append(send(piece, piece, partner))

    for h in (0, 1):
        gf[c, h, last_at(h, 0, 0)] = g2[48 * h : 48 * h + 48]
    step = {}
    for d in order:
        for h in (0, 1):
            piece = gf.at[c, h, last_at(h, 0, 0)]
            step[d, h] = send(piece, piece, (ypeer, xpeer)[h](d))
    for h in (0, 1):
        onward(h, 0)
    for copy in back:
        copy.wait_recv()
    swap.append(send(gd.at[c], gd.at[c], partner))
    for n in (1, 3, 2):
        for h in (0, 1):
            step[n, h].wait_recv()
            onward(h, n)
    for n in (0, 1, 3, 2):
        for d in (1, 3, 2):
            for h in (0, 1):
                gathered[n, d, h].wait_recv()
                piece = gf.at[c, h, last_at(h, d, n)]
                swap.append(send(piece, piece, partner))
    for copy in swap:
        copy.wait_recv()
    sent += list(step.values()) + list(gathered.values()) + swap
    norm = jnp.zeros((1, 1), f32)
    for tick in range(4):
        for core in range(2):
            rows = slice(256 * tick + 128 * core, 256 * tick + 128 * core + 128)
            block = jnp.concatenate([gd[core, h, :, tick].reshape(128, 128) for h in (0, 1)], axis=1)
            norm = norm + jnp.sum(jnp.sum(block * block, axis=0, keepdims=True), axis=1, keepdims=True)
            high, low = split(block)
            gc[tick, rows] = block
            gch[tick, rows] = high
            gcl[tick, rows] = low
    for core in range(2):
        for k in range(3):
            a, b = pairs[core][k]
            block = jnp.concatenate(
                [gf[core, h, 256 * k : 256 * k + 256] for h in (0, 1)], axis=1
            )
            square = jnp.sum(jnp.sum(block * block, axis=0, keepdims=True), axis=1, keepdims=True)
            norm = norm + 2.0 * square
            high, low = split(block)
            gc[b, 256 * a : 256 * a + 256] = block
            gch[b, 256 * a : 256 * a + 256] = high
            gcl[b, 256 * a : 256 * a + 256] = low
            block = block.T
            high, low = split(block)
            gc[a, 256 * b : 256 * b + 256] = block
            gch[a, 256 * b : 256 * b + 256] = high
            gcl[a, 256 * b : 256 * b + 256] = low
    factor = 2.0 / jnp.sqrt(norm + jnp.float32(1e-06))

    row = lax.broadcasted_iota(jnp.int32, (1024, 256), 0)
    col = lax.broadcasted_iota(jnp.int32, (1024, 256), 1)
    va[...] = jnp.where(row == col + 256 * t, 1.0, 0.0)
    vb[...] = factor * gc[t] - va[...]
    acc[...] = coefs[0] * va[...] + coefs[1] * vb[...]
    older, newer = va, vb
    for degree in (2, 3, 4):
        high, low = split(newer[...])
        vh[...] = high
        vl[...] = low
        for i in range(4):
            rows = slice(256 * i, 256 * i + 256)
            image = jnp.zeros((256, 256), f32)
            for k in range(4):
                kk = slice(256 * k, 256 * k + 256)
                image = image + (
                    dot(gch[k, rows], vh[kk])
                    + (dot(gch[k, rows], vl[kk]) + dot(gcl[k, rows], vh[kk]))
                )
            following = 2.0 * (factor * image - newer[rows]) - older[rows]
            acc[rows] = acc[rows] + coefs[degree] * following
            older[rows] = following
        older, newer = newer, older

    for copy, _, there in rest[early:]:
        pl.when(there)(copy.wait_recv)
    for a in range(4):
        high, low = split(wf[a])
        wfh[a] = high
        wfl[a] = low
    high, low = split(acc[...])
    vh[...] = high
    vl[...] = low
    for i in range(2):
        rows = slice(256 * i, 256 * i + 256)
        lowrank = jnp.zeros((256, 256), f32)
        for k in range(4):
            kk = slice(256 * k, 256 * k + 256)
            lowrank = lowrank + (
                dot(wfh[k, rows], vh[kk])
                + (dot(wfh[k, rows], vl[kk]) + dot(wfl[k, rows], vh[kk]))
            )
        low_out[rows] = 0.5 * lowrank
    for copy in sent:
        copy.wait_send()
    for copy, here, _ in rest:
        pl.when(here)(copy.wait_send)


copies = 1 + 6 + 6 + 7 + 6 + 6 + 1 + 3 + 4 + 15 + 24 + 6 + 7 + 3 + 6 + 24 + 32


def on_device(telemetry, sparse, multiplier):
    block = jax.ShapeDtypeStruct((512, 256), f32)
    vmem = pl.BlockSpec(memory_space=pltpu.VMEM)
    half = pl.pallas_call(
        kernel,
        out_shape=block,
        in_specs=[pl.BlockSpec(memory_space=pltpu.HBM)] * 3,
        out_specs=vmem,
        scratch_shapes=[
            pltpu.VMEM((4, 512, 256), f32),
            pltpu.VMEM((4, 128, 256), f32),
            pltpu.VMEM((512, 256), bf16),
            pltpu.VMEM((512, 256), bf16),
            pltpu.VMEM((2, 256, 128), f32),
            pltpu.VMEM((2, 128, 128), f32),
            pltpu.VMEM((2, 3, 32, 128), f32),
            pltpu.VMEM((2, 32, 128), f32),
            pltpu.VMEM((2, 3, 8, 128), f32),
            pltpu.VMEM((2, 8, 128), f32),
            pltpu.VMEM((2, 4, 2, 8, 128), f32),
            pltpu.VMEM((2, 2, 16, 4, 8, 128), f32),
            pltpu.VMEM((4, 256, 256), bf16),
            pltpu.VMEM((4, 256, 256), bf16),
            pltpu.VMEM((2, 768, 128), f32),
            pltpu.VMEM((2, 3, 4, 48, 128), f32),
            pltpu.VMEM((2, 3, 48, 128), f32),
            pltpu.VMEM((2, 3, 48, 128), f32),
            pltpu.VMEM((96, 128), f32),
            pltpu.VMEM((2, 4, 24, 128), f32),
            pltpu.VMEM((96, 128), f32),
            pltpu.VMEM((2, 2, 768, 128), f32),
            pltpu.VMEM((4, 1024, 256), f32),
            pltpu.VMEM((4, 1024, 256), bf16),
            pltpu.VMEM((4, 1024, 256), bf16),
            pltpu.VMEM((1024, 256), f32),
            pltpu.VMEM((1024, 256), f32),
            pltpu.VMEM((1024, 256), bf16),
            pltpu.VMEM((1024, 256), bf16),
            pltpu.VMEM((1024, 256), f32),
            pltpu.VMEM((4, 512, 256), bf16),
            pltpu.VMEM((4, 512, 256), bf16),
            pltpu.VMEM((512, 256), f32),
            pltpu.VMEM((512, 256), f32),
            pltpu.VMEM((512, 256), f32),
            pltpu.SemaphoreType.DMA((3,)),
            pltpu.SemaphoreType.DMA((copies,)),
            pltpu.SemaphoreType.DMA((copies,)),
        ],
        compiler_params=pltpu.CompilerParams(
            collective_id=0, has_side_effects=True, vmem_limit_bytes=56 << 20
        ),
    )(telemetry, sparse, multiplier)
    lowrank = 2.0 * half
    level = telemetry - lowrank + multiplier
    size = jnp.maximum(jnp.abs(level) - shrink_level, 0.0)
    new_sparse = jnp.where(level < 0.0, -size, size)
    return lowrank, new_sparse, multiplier + telemetry - lowrank - new_sparse


def solution(mesh):
    spec = P("series", "tick")
    return jax.shard_map(
        on_device,
        mesh=mesh,
        in_specs=(spec, spec, spec),
        out_specs=(spec, spec, spec),
        check_vma=False,
    )
```

```python
import functools

import jax
import jax.numpy as jnp
from jax import lax
from jax.experimental import pallas as pl
from jax.experimental.pallas import tpu as pltpu
from jax.sharding import PartitionSpec as P

MESH = pl.DeviceIdType.MESH
coefs = (0.4, 0.5, 0.1, -0.04, -0.06)
shrink_level = 0.5
f32, bf16 = jnp.float32, jnp.bfloat16

pairs = (((0, 1), (0, 2), (0, 3)), ((1, 2), (1, 3), (2, 3)))


def split(value):
    high = value.astype(bf16)
    return high, (value - high.astype(f32)).astype(bf16)


def dot(a, b, dims=((1,), (0,))):
    return lax.dot_general(a, b, (dims, ((), ())), preferred_element_type=f32)


def kernel(
    tele_in, sparse_in, mult_in, low_out,
    wf, wp, dh, dl, dpart, dother, dr1, ds1, dr2, ds2, drz, gd, gh, gl, part, r1, s1, r2, s2, r3, g2, gf,
    gc, gch, gcl, va, vb, vh, vl, acc, wfh, wfl, tele, sparse, mult, ls, ss, rs,
):
    series, t = lax.axis_index("series"), lax.axis_index("tick")
    c = series % 2
    x = (series // 2) % 4
    y = (series // 8) % 4
    zh = series // 32

    def at(zh_, t_, y_, x_, c_):
        return ((zh_ * 4 + y_) * 4 + x_) * 2 + c_, t_

    def xpeer(d):
        return at(zh, t, y, (x + d) % 4, c)

    def ypeer(d):
        return at(zh, t, (y + d) % 4, x, c)

    def zpeer(dh, d):
        return at((zh + dh) % 2, (t + d) % 4, y, x, c)

    partner = at(zh, t, y, x, 1 - c)
    count = [0]

    def send(src, dst, device, here=None):
        k = count[0]
        count[0] += 1
        copy = pltpu.make_async_remote_copy(
            src_ref=src, dst_ref=dst, send_sem=ss.at[k], recv_sem=rs.at[k],
            device_id=device, device_id_type=MESH,
        )
        if here is None:
            copy.start()
        else:
            pl.when(here)(copy.start)
        return copy

    sent = []

    loads = [
        pltpu.make_async_copy(src, dst, ls.at[i])
        for i, (src, dst) in enumerate(((tele_in, tele), (sparse_in, sparse), (mult_in, mult)))
    ]
    for load in loads:
        load.start()
    barrier = pltpu.get_barrier_semaphore()
    peers = [xpeer(d) for d in (1, 2, 3)] + [ypeer(d) for d in (1, 2, 3)]
    peers += [zpeer(dh, d) for dh in (0, 1) for d in range(4) if dh or d] + [partner]
    for p in peers:
        pl.semaphore_signal(barrier, inc=1, device_id=p, device_id_type=MESH)
    for load in loads:
        load.wait()
    wf[t] = tele[...] - sparse[...] + mult[...]
    pl.semaphore_wait(barrier, len(peers))

    first = []
    for d in (1, 2, 3):
        q = (t + d) % 4
        block = wf.at[t, pl.ds(128 * q, 128)]
        first.append(send(block, block, zpeer(0, d)))
    middle = (t - 1) * (t - 2) == 0
    ends = (t - 1) * (t - 2) != 0
    side = 1 - t // 2
    rest = []

    def spread(d, e, early=None):
        q = (t + d) % 4
        block = wf.at[t, pl.ds(128 * ((q + e) % 4), 128)]
        here, there = {1: (t != 3, t != 0), 2: (ends, middle), 3: (t != 0, t != 3)}[d]
        copy = send(block, block, zpeer(0, d), here if early is None else early)
        rest.append((copy, here, there))
        return copy

    def relay(o, r):
        block = wf.at[o, pl.ds(128 * r, 128)]
        rest.append((send(block, block, at(zh, 3 * (t // 2), y, x, c), middle), middle, ends))

    near = [spread(1, 2, t % 2 == 0), spread(3, 1, t % 2 == 1)]
    mine = pl.ds(pl.multiple_of(128 * t, 128), 128)
    passed = [send(wf.at[t, mine], wp.at[t], partner)]

    order = (2, 1, 3)
    cols = ((0,), (0,))
    high, low = split(wf[t])
    dh[...] = high
    dl[...] = low
    block = dot(dh[...], dh[...], cols) + (dot(dh[...], dl[...], cols) + dot(dl[...], dh[...], cols))
    for h in (0, 1):
        dpart[h] = block[:, 128 * h : 128 * h + 128]
    low_half = pl.ds(pl.multiple_of(128 * c, 128), 128)
    high_half = pl.ds(pl.multiple_of(128 * (1 - c), 128), 128)
    cross = send(dpart.at[:, high_half], dother, partner)
    cross.wait_recv()
    for h in (0, 1):
        dother[h] = dpart[h, low_half] + dother[h]
    step = {}
    for d in order:
        step[d, 0] = send(dother.at[0, pl.ds(32 * ((x + d) % 4), 32)], dr1.at[0, d - 1], xpeer(d))
        step[d, 1] = send(dother.at[1, pl.ds(32 * ((y + d) % 4), 32)], dr1.at[1, d - 1], ypeer(d))
    step2 = {}
    for h, i in ((0, x), (1, y)):
        for d in order:
            step[d, h].wait_recv()
        own = dother[h, pl.ds(pl.multiple_of(32 * i, 32), 32)]
        ds1[h] = (own + dr1[h, 0]) + (dr1[h, 1] + dr1[h, 2])
        i, peer = ((y, ypeer), (x, xpeer))[h]
        for d in order:
            step2[d, h] = send(ds1.at[h, pl.ds(8 * ((i + d) % 4), 8)], dr2.at[h, d - 1], peer(d))
    sent += [cross] + list(step.values()) + list(step2.values())

    for d in (1, 2, 3):
        first[d - 1].wait_recv()
        o = (t - d + 4) % 4
        passed.append(send(wf.at[o, mine], wp.at[o], partner))
    sent += first + passed
    for h, i in ((0, y), (1, x)):
        for d in order:
            step2[d, h].wait_recv()
        own = ds1[h, pl.ds(pl.multiple_of(8 * i, 8), 8)]
        ds2[h] = (own + dr2[h, 0]) + (dr2[h, 1] + dr2[h, 2])

    along = []
    for flip in (1, 0):
        for d in (0, 2, 1, 3):
            if flip or d:
                along.append(send(ds2, drz.at[zh, t], zpeer(flip, d)))
    drz[zh, t] = ds2[...]
    sent += along
    pl.when(t == 1)(near[0].start)
    pl.when(t == 2)(near[1].start)
    relay(3 * side, t)
    relay((3 - t) % 4, t)
    for k in (0, 1):
        spread(2, (k + side) % 3 + 1)
    spread(1, 3)
    spread(3, 2)

    for a in range(4):
        high, low = split(wf[a, mine])
        gh[a, 0:128] = high
        gl[a, 0:128] = low
    for copy in passed:
        copy.wait_recv()
    for a in range(4):
        high, low = split(wp[a])
        gh[a, 128:256] = high
        gl[a, 128:256] = low
    for k in range(3):
        (a0, b0), (a1, b1) = pairs[0][k], pairs[1][k]
        a, b = a0 + c * (a1 - a0), b0 + c * (b1 - b0)
        rows = ((0,), (0,))
        block = dot(gh[a], gh[b], rows) + (dot(gh[a], gl[b], rows) + dot(gl[a], gh[b], rows))
        part[0, 256 * k : 256 * k + 256] = block[:, :128]
        part[1, 256 * k : 256 * k + 256] = block[:, 128:]

    def first_at(h, i, n):
        return pl.ds(pl.multiple_of(192 * i + 48 * ((((y, x)[h]) + n) % 4), 48), 48)

    step = {}
    for n in order + (0,):
        for d in order:
            for h in (0, 1):
                i, peer = ((x, xpeer), (y, ypeer))[h]
                step[n, d, h] = send(part.at[h, first_at(h, (i + d) % 4, n)], r1.at[h, d - 1, n], peer(d))
    step2 = {}
    for n in order + (0,):
        for h in (0, 1):
            i, peer = ((x, ypeer), (y, xpeer))[h]
            for d in order:
                step[n, d, h].wait_recv()
            value = (part[h, first_at(h, i, n)] + r1[h, 0, n]) + (r1[h, 1, n] + r1[h, 2, n])
            if n:
                s1[h, n - 1] = value
                step2[n, h] = send(s1.at[h, n - 1], r2.at[h, n - 1], peer(n))
            else:
                s2[48 * h : 48 * h + 48] = value
    sent += list(step.values()) + list(step2.values())
    for copy in along:
        copy.wait_recv()
    back = []
    for h, i, peer in ((0, 4 * x + y, ypeer), (1, 4 * y + x, xpeer)):
        for tick in range(4):
            gd[c, h, i, tick] = drz[0, tick, h] + drz[1, tick, h]
        for d in order:
            back.append(send(gd.at[c, h, i], gd.at[c, h, i], peer(d)))
    sent += back
    for h in (0, 1):
        for n in order:
            step2[n, h].wait_recv()
        rows = slice(48 * h, 48 * h + 48)
        s2[rows] = (s2[rows] + r2[h, 0]) + (r2[h, 1] + r2[h, 2])

    step = []
    for dh in (1, 0):
        for d in (0, 2, 1, 3):
            if dh or d:
                step.append(send(s2.at[pl.ds(24 * ((t + d) % 4), 24)], r3.at[zh, t], zpeer(dh, d)))
    chunk = pl.ds(pl.multiple_of(24 * t, 24), 24)
    r3[zh, t] = s2[chunk]
    for copy in back:
        copy.wait_recv()
    back = []
    for h, i, peer in ((0, x, xpeer), (1, y, ypeer)):
        row = gd.at[c, h, pl.ds(4 * i, 4)]
        for d in order:
            back.append(send(row, row, peer(d)))
    sent += back
    for copy in step:
        copy.wait_recv()
    sent += step
    total = r3[0, 0]
    for i in range(1, 8):
        total = total + r3[i // 4, i % 4]
    g2[chunk] = total

    step = []
    for d in (1, 2, 3):
        step.append(send(g2.at[chunk], g2.at[chunk], zpeer(0, d)))
    for copy in step:
        copy.wait_recv()
    sent += step
    early = len(rest)
    for copy, _, there in rest:
        pl.when(there)(copy.wait_recv)
    for k in (0, 1):
        relay(3 * side, 2 * side + k)
        relay((3 - t) % 4, 2 * side + k)
    spread(2, (2 + side) % 3 + 1)
    spread(1, 1)
    spread(3, 3)
    def last_at(h, d, n):
        own = (192 * ((x - d + 4) % 4) + 48 * ((y - n + 4) % 4), 192 * ((y - d + 4) % 4) + 48 * ((x - n + 4) % 4))[h]
        return pl.ds(pl.multiple_of(own, 48), 48)

    gathered, swap = {}, []

    def onward(h, n):
        piece = gf.at[c, h, last_at(h, 0, n)]
        for d in order:
            gathered[n, d, h] = send(piece, piece, (xpeer, ypeer)[h](d))

    for h in (0, 1):
        gf[c, h, last_at(h, 0, 0)] = g2[48 * h : 48 * h + 48]
    step = {}
    for d in order:
        for h in (0, 1):
            piece = gf.at[c, h, last_at(h, 0, 0)]
            step[d, h] = send(piece, piece, (ypeer, xpeer)[h](d))
    for h in (0, 1):
        onward(h, 0)
    for copy in back:
        copy.wait_recv()
    swap.append(send(gd.at[c], gd.at[c], partner))
    for n in (1, 3, 2):
        for h in (0, 1):
            step[n, h].wait_recv()
            onward(h, n)
    for d in (0, 1, 3, 2):
        for h in (0, 1):
            if d:
                for n in (0, 1, 3, 2):
                    gathered[n, d, h].wait_recv()
            row = gf.at[c, h, pl.ds(192 * (((x, y)[h] - d + 4) % 4), 192)]
            swap.append(send(row, row, partner))
    for copy in swap:
        copy.wait_recv()
    sent += list(step.values()) + list(gathered.values()) + swap
    norm = jnp.zeros((1, 1), f32)
    for tick in range(4):
        for core in range(2):
            rows = slice(256 * tick + 128 * core, 256 * tick + 128 * core + 128)
            block = jnp.concatenate([gd[core, h, :, tick].reshape(128, 128) for h in (0, 1)], axis=1)
            norm = norm + jnp.sum(jnp.sum(block * block, axis=0, keepdims=True), axis=1, keepdims=True)
            high, low = split(block)
            gc[tick, rows] = block
            gch[tick, rows] = high
            gcl[tick, rows] = low
    for core in range(2):
        for k in range(3):
            a, b = pairs[core][k]
            block = jnp.concatenate(
                [gf[core, h, 256 * k : 256 * k + 256] for h in (0, 1)], axis=1
            )
            square = jnp.sum(jnp.sum(block * block, axis=0, keepdims=True), axis=1, keepdims=True)
            norm = norm + 2.0 * square
            high, low = split(block)
            gc[b, 256 * a : 256 * a + 256] = block
            gch[b, 256 * a : 256 * a + 256] = high
            gcl[b, 256 * a : 256 * a + 256] = low
            block = block.T
            high, low = split(block)
            gc[a, 256 * b : 256 * b + 256] = block
            gch[a, 256 * b : 256 * b + 256] = high
            gcl[a, 256 * b : 256 * b + 256] = low
    factor = 2.0 / jnp.sqrt(norm + jnp.float32(1e-06))

    row = lax.broadcasted_iota(jnp.int32, (1024, 256), 0)
    col = lax.broadcasted_iota(jnp.int32, (1024, 256), 1)
    va[...] = jnp.where(row == col + 256 * t, 1.0, 0.0)
    vb[...] = factor * gc[t] - va[...]
    acc[...] = coefs[0] * va[...] + coefs[1] * vb[...]
    older, newer = va, vb
    for degree in (2, 3, 4):
        high, low = split(newer[...])
        vh[...] = high
        vl[...] = low
        for i in range(4):
            rows = slice(256 * i, 256 * i + 256)
            image = jnp.zeros((256, 256), f32)
            for k in range(4):
                kk = slice(256 * k, 256 * k + 256)
                image = image + (
                    dot(gch[k, rows], vh[kk])
                    + (dot(gch[k, rows], vl[kk]) + dot(gcl[k, rows], vh[kk]))
                )
            following = 2.0 * (factor * image - newer[rows]) - older[rows]
            acc[rows] = acc[rows] + coefs[degree] * following
            older[rows] = following
        older, newer = newer, older

    for copy, _, there in rest[early:]:
        pl.when(there)(copy.wait_recv)
    for a in range(4):
        high, low = split(wf[a])
        wfh[a] = high
        wfl[a] = low
    high, low = split(acc[...])
    vh[...] = high
    vl[...] = low
    for i in range(2):
        rows = slice(256 * i, 256 * i + 256)
        lowrank = jnp.zeros((256, 256), f32)
        for k in range(4):
            kk = slice(256 * k, 256 * k + 256)
            lowrank = lowrank + (
                dot(wfh[k, rows], vh[kk])
                + (dot(wfh[k, rows], vl[kk]) + dot(wfl[k, rows], vh[kk]))
            )
        low_out[rows] = 0.5 * lowrank
    for copy in sent:
        copy.wait_send()
    for copy, here, _ in rest:
        pl.when(here)(copy.wait_send)


copies = 1 + 6 + 6 + 7 + 6 + 6 + 1 + 3 + 4 + 15 + 24 + 6 + 7 + 3 + 6 + 24 + 8


def on_device(telemetry, sparse, multiplier):
    block = jax.ShapeDtypeStruct((512, 256), f32)
    vmem = pl.BlockSpec(memory_space=pltpu.VMEM)
    half = pl.pallas_call(
        kernel,
        out_shape=block,
        in_specs=[pl.BlockSpec(memory_space=pltpu.HBM)] * 3,
        out_specs=vmem,
        scratch_shapes=[
            pltpu.VMEM((4, 512, 256), f32),
            pltpu.VMEM((4, 128, 256), f32),
            pltpu.VMEM((512, 256), bf16),
            pltpu.VMEM((512, 256), bf16),
            pltpu.VMEM((2, 256, 128), f32),
            pltpu.VMEM((2, 128, 128), f32),
            pltpu.VMEM((2, 3, 32, 128), f32),
            pltpu.VMEM((2, 32, 128), f32),
            pltpu.VMEM((2, 3, 8, 128), f32),
            pltpu.VMEM((2, 8, 128), f32),
            pltpu.VMEM((2, 4, 2, 8, 128), f32),
            pltpu.VMEM((2, 2, 16, 4, 8, 128), f32),
            pltpu.VMEM((4, 256, 256), bf16),
            pltpu.VMEM((4, 256, 256), bf16),
            pltpu.VMEM((2, 768, 128), f32),
            pltpu.VMEM((2, 3, 4, 48, 128), f32),
            pltpu.VMEM((2, 3, 48, 128), f32),
            pltpu.VMEM((2, 3, 48, 128), f32),
            pltpu.VMEM((96, 128), f32),
            pltpu.VMEM((2, 4, 24, 128), f32),
            pltpu.VMEM((96, 128), f32),
            pltpu.VMEM((2, 2, 768, 128), f32),
            pltpu.VMEM((4, 1024, 256), f32),
            pltpu.VMEM((4, 1024, 256), bf16),
            pltpu.VMEM((4, 1024, 256), bf16),
            pltpu.VMEM((1024, 256), f32),
            pltpu.VMEM((1024, 256), f32),
            pltpu.VMEM((1024, 256), bf16),
            pltpu.VMEM((1024, 256), bf16),
            pltpu.VMEM((1024, 256), f32),
            pltpu.VMEM((4, 512, 256), bf16),
            pltpu.VMEM((4, 512, 256), bf16),
            pltpu.VMEM((512, 256), f32),
            pltpu.VMEM((512, 256), f32),
            pltpu.VMEM((512, 256), f32),
            pltpu.SemaphoreType.DMA((3,)),
            pltpu.SemaphoreType.DMA((copies,)),
            pltpu.SemaphoreType.DMA((copies,)),
        ],
        compiler_params=pltpu.CompilerParams(
            collective_id=0, has_side_effects=True, vmem_limit_bytes=56 << 20
        ),
    )(telemetry, sparse, multiplier)
    lowrank = 2.0 * half
    level = telemetry - lowrank + multiplier
    size = jnp.maximum(jnp.abs(level) - shrink_level, 0.0)
    new_sparse = jnp.where(level < 0.0, -size, size)
    return lowrank, new_sparse, multiplier + telemetry - lowrank - new_sparse


def solution(mesh):
    spec = P("series", "tick")
    return jax.shard_map(
        on_device,
        mesh=mesh,
        in_specs=(spec, spec, spec),
        out_specs=(spec, spec, spec),
        check_vma=False,
    )
```

```python
import functools

import jax
import jax.numpy as jnp
from jax import lax
from jax.experimental import pallas as pl
from jax.experimental.pallas import tpu as pltpu
from jax.sharding import PartitionSpec as P

MESH = pl.DeviceIdType.MESH
coefs = (0.4, 0.5, 0.1, -0.04, -0.06)
shrink_level = 0.5
f32, bf16 = jnp.float32, jnp.bfloat16

pairs = (((0, 1), (0, 2), (0, 3)), ((1, 2), (1, 3), (2, 3)))


def split(value):
    high = value.astype(bf16)
    return high, (value - high.astype(f32)).astype(bf16)


def dot(a, b, dims=((1,), (0,))):
    return lax.dot_general(a, b, (dims, ((), ())), preferred_element_type=f32)


def product(high, low, other_high, other_low):
    return dot(high, other_high) + (dot(high, other_low) + dot(low, other_high))


def kernel(
    tele_in, sparse_in, mult_in, low_out,
    wf, wp, dh, dl, dpart, dother, dr1, ds1, dr2, ds2, drz, gd, gh, gl, part, r1, s1, r2, s2, r3, g2, gf,
    gc, gch, gcl, va, vb, vh, vl, acc, wfh, wfl, tele, sparse, mult, ls, ss, rs,
):
    series, t = lax.axis_index("series"), lax.axis_index("tick")
    c = series % 2
    x = (series // 2) % 4
    y = (series // 8) % 4
    zh = series // 32

    def at(zh_, t_, y_, x_, c_):
        return ((zh_ * 4 + y_) * 4 + x_) * 2 + c_, t_

    def xpeer(d):
        return at(zh, t, y, (x + d) % 4, c)

    def ypeer(d):
        return at(zh, t, (y + d) % 4, x, c)

    def zpeer(dh, d):
        return at((zh + dh) % 2, (t + d) % 4, y, x, c)

    partner = at(zh, t, y, x, 1 - c)
    count = [0]

    def send(src, dst, device, here=None):
        k = count[0]
        count[0] += 1
        copy = pltpu.make_async_remote_copy(
            src_ref=src, dst_ref=dst, send_sem=ss.at[k], recv_sem=rs.at[k],
            device_id=device, device_id_type=MESH,
        )
        if here is None:
            copy.start()
        else:
            pl.when(here)(copy.start)
        return copy

    sent = []

    loads = [
        pltpu.make_async_copy(src, dst, ls.at[i])
        for i, (src, dst) in enumerate(((tele_in, tele), (sparse_in, sparse), (mult_in, mult)))
    ]
    for load in loads:
        load.start()
    barrier = pltpu.get_barrier_semaphore()
    peers = [xpeer(d) for d in (1, 2, 3)] + [ypeer(d) for d in (1, 2, 3)]
    peers += [zpeer(dh, d) for dh in (0, 1) for d in range(4) if dh or d] + [partner]
    for p in peers:
        pl.semaphore_signal(barrier, inc=1, device_id=p, device_id_type=MESH)
    for load in loads:
        load.wait()
    wf[t] = tele[...] - sparse[...] + mult[...]
    pl.semaphore_wait(barrier, len(peers))

    first = []
    for d in (1, 2, 3):
        q = (t + d) % 4
        block = wf.at[t, pl.ds(128 * q, 128)]
        first.append(send(block, block, zpeer(0, d)))
    middle = (t - 1) * (t - 2) == 0
    ends = (t - 1) * (t - 2) != 0
    side = 1 - t // 2
    rest = []

    def spread(d, e, early=None):
        q = (t + d) % 4
        block = wf.at[t, pl.ds(128 * ((q + e) % 4), 128)]
        here, there = {1: (t != 3, t != 0), 2: (ends, middle), 3: (t != 0, t != 3)}[d]
        copy = send(block, block, zpeer(0, d), here if early is None else early)
        rest.append((copy, here, there))
        return copy

    def relay(o, r):
        block = wf.at[o, pl.ds(128 * r, 128)]
        rest.append((send(block, block, at(zh, 3 * (t // 2), y, x, c), middle), middle, ends))

    near = [spread(1, 2, t % 2 == 0), spread(3, 1, t % 2 == 1)]
    mine = pl.ds(pl.multiple_of(128 * t, 128), 128)
    passed = [send(wf.at[t, mine], wp.at[t], partner)]

    order = (2, 1, 3)
    cols = ((0,), (0,))
    high, low = split(wf[t])
    dh[...] = high
    dl[...] = low
    block = dot(dh[...], dh[...], cols) + (dot(dh[...], dl[...], cols) + dot(dl[...], dh[...], cols))
    for h in (0, 1):
        dpart[h] = block[:, 128 * h : 128 * h + 128]
    low_half = pl.ds(pl.multiple_of(128 * c, 128), 128)
    high_half = pl.ds(pl.multiple_of(128 * (1 - c), 128), 128)
    cross = send(dpart.at[:, high_half], dother, partner)
    cross.wait_recv()
    for h in (0, 1):
        dother[h] = dpart[h, low_half] + dother[h]
    step = {}
    for d in order:
        step[d, 0] = send(dother.at[0, pl.ds(32 * ((x + d) % 4), 32)], dr1.at[0, d - 1], xpeer(d))
        step[d, 1] = send(dother.at[1, pl.ds(32 * ((y + d) % 4), 32)], dr1.at[1, d - 1], ypeer(d))
    step2 = {}
    for h, i in ((0, x), (1, y)):
        for d in order:
            step[d, h].wait_recv()
        own = dother[h, pl.ds(pl.multiple_of(32 * i, 32), 32)]
        ds1[h] = (own + dr1[h, 0]) + (dr1[h, 1] + dr1[h, 2])
        i, peer = ((y, ypeer), (x, xpeer))[h]
        for d in order:
            step2[d, h] = send(ds1.at[h, pl.ds(8 * ((i + d) % 4), 8)], dr2.at[h, d - 1], peer(d))
    sent += [cross] + list(step.values()) + list(step2.values())

    for d in (1, 2, 3):
        first[d - 1].wait_recv()
        o = (t - d + 4) % 4
        passed.append(send(wf.at[o, mine], wp.at[o], partner))
    sent += first + passed
    for h, i in ((0, y), (1, x)):
        for d in order:
            step2[d, h].wait_recv()
        own = ds1[h, pl.ds(pl.multiple_of(8 * i, 8), 8)]
        ds2[h] = (own + dr2[h, 0]) + (dr2[h, 1] + dr2[h, 2])

    along = []
    for flip in (1, 0):
        for d in (0, 2, 1, 3):
            if flip or d:
                along.append(send(ds2, drz.at[zh, t], zpeer(flip, d)))
    drz[zh, t] = ds2[...]
    sent += along
    pl.when(t == 1)(near[0].start)
    pl.when(t == 2)(near[1].start)
    relay(3 * side, t)
    relay((3 - t) % 4, t)
    for k in (0, 1):
        spread(2, (k + side) % 3 + 1)
    spread(1, 3)
    spread(3, 2)

    for a in range(4):
        high, low = split(wf[a, mine])
        gh[a, 0:128] = high
        gl[a, 0:128] = low
    for copy in passed:
        copy.wait_recv()
    for a in range(4):
        high, low = split(wp[a])
        gh[a, 128:256] = high
        gl[a, 128:256] = low
    for k in range(3):
        (a0, b0), (a1, b1) = pairs[0][k], pairs[1][k]
        a, b = a0 + c * (a1 - a0), b0 + c * (b1 - b0)
        rows = ((0,), (0,))
        block = dot(gh[a], gh[b], rows) + (dot(gh[a], gl[b], rows) + dot(gl[a], gh[b], rows))
        part[0, 256 * k : 256 * k + 256] = block[:, :128]
        part[1, 256 * k : 256 * k + 256] = block[:, 128:]

    def first_at(h, i, n):
        return pl.ds(pl.multiple_of(192 * i + 48 * ((((y, x)[h]) + n) % 4), 48), 48)

    step = {}
    for n in order + (0,):
        for d in order:
            for h in (0, 1):
                i, peer = ((x, xpeer), (y, ypeer))[h]
                step[n, d, h] = send(part.at[h, first_at(h, (i + d) % 4, n)], r1.at[h, d - 1, n], peer(d))
    step2 = {}
    for n in order + (0,):
        for h in (0, 1):
            i, peer = ((x, ypeer), (y, xpeer))[h]
            for d in order:
                step[n, d, h].wait_recv()
            value = (part[h, first_at(h, i, n)] + r1[h, 0, n]) + (r1[h, 1, n] + r1[h, 2, n])
            if n:
                s1[h, n - 1] = value
                step2[n, h] = send(s1.at[h, n - 1], r2.at[h, n - 1], peer(n))
            else:
                s2[48 * h : 48 * h + 48] = value
    sent += list(step.values()) + list(step2.values())
    for copy in along:
        copy.wait_recv()
    back = []
    for h, i, peer in ((0, 4 * x + y, ypeer), (1, 4 * y + x, xpeer)):
        for tick in range(4):
            gd[c, h, i, tick] = drz[0, tick, h] + drz[1, tick, h]
        for d in order:
            back.append(send(gd.at[c, h, i], gd.at[c, h, i], peer(d)))
    sent += back
    for h in (0, 1):
        for n in order:
            step2[n, h].wait_recv()
        rows = slice(48 * h, 48 * h + 48)
        s2[rows] = (s2[rows] + r2[h, 0]) + (r2[h, 1] + r2[h, 2])

    step = []
    for dh in (1, 0):
        for d in (0, 2, 1, 3):
            if dh or d:
                step.append(send(s2.at[pl.ds(24 * ((t + d) % 4), 24)], r3.at[zh, t], zpeer(dh, d)))
    third = [spread(1, 1, t % 2 == 0), spread(3, 3, t % 2 == 1)]
    held = rest[-2:]
    del rest[-2:]
    chunk = pl.ds(pl.multiple_of(24 * t, 24), 24)
    r3[zh, t] = s2[chunk]
    for copy in back:
        copy.wait_recv()
    back = []
    for h, i, peer in ((0, x, xpeer), (1, y, ypeer)):
        row = gd.at[c, h, pl.ds(4 * i, 4)]
        for d in order:
            back.append(send(row, row, peer(d)))
    sent += back
    for copy in step:
        copy.wait_recv()
    sent += step
    total = r3[0, 0]
    for i in range(1, 8):
        total = total + r3[i // 4, i % 4]
    g2[chunk] = total

    step = []
    for d in (1, 2, 3):
        step.append(send(g2.at[chunk], g2.at[chunk], zpeer(0, d)))
    for copy in step:
        copy.wait_recv()
    sent += step
    early = len(rest)
    for copy, _, there in rest:
        pl.when(there)(copy.wait_recv)
    for k in (0, 1):
        relay(3 * side, 2 * side + k)
        relay((3 - t) % 4, 2 * side + k)
    spread(2, (2 + side) % 3 + 1)
    pl.when(t == 1)(third[0].start)
    pl.when(t == 2)(third[1].start)
    rest += held
    def last_at(h, d, n):
        own = (192 * ((x - d + 4) % 4) + 48 * ((y - n + 4) % 4), 192 * ((y - d + 4) % 4) + 48 * ((x - n + 4) % 4))[h]
        return pl.ds(pl.multiple_of(own, 48), 48)

    gathered, swap = {}, []

    def onward(h, n):
        piece = gf.at[c, h, last_at(h, 0, n)]
        for d in order:
            gathered[n, d, h] = send(piece, piece, (xpeer, ypeer)[h](d))

    for h in (0, 1):
        gf[c, h, last_at(h, 0, 0)] = g2[48 * h : 48 * h + 48]
    step = {}
    for d in order:
        for h in (0, 1):
            piece = gf.at[c, h, last_at(h, 0, 0)]
            step[d, h] = send(piece, piece, (ypeer, xpeer)[h](d))
    for h in (0, 1):
        onward(h, 0)
    for copy in back:
        copy.wait_recv()
    swap.append(send(gd.at[c], gd.at[c], partner))
    for n in (1, 3, 2):
        for h in (0, 1):
            step[n, h].wait_recv()
            onward(h, n)
    for d in (0, 1, 3, 2):
        for h in (0, 1):
            if d:
                for n in (0, 1, 3, 2):
                    gathered[n, d, h].wait_recv()
            row = gf.at[c, h, pl.ds(192 * (((x, y)[h] - d + 4) % 4), 192)]
            swap.append(send(row, row, partner))
    for copy in swap:
        copy.wait_recv()
    sent += list(step.values()) + list(gathered.values()) + swap
    norm = jnp.zeros((1, 1), f32)
    for tick in range(4):
        for core in range(2):
            rows = slice(256 * tick + 128 * core, 256 * tick + 128 * core + 128)
            block = jnp.concatenate([gd[core, h, :, tick].reshape(128, 128) for h in (0, 1)], axis=1)
            norm = norm + jnp.sum(jnp.sum(block * block, axis=0, keepdims=True), axis=1, keepdims=True)
            high, low = split(block)
            gc[tick, rows] = block
            gch[rows, 256 * tick : 256 * tick + 256] = high
            gcl[rows, 256 * tick : 256 * tick + 256] = low
    for core in range(2):
        for k in range(3):
            a, b = pairs[core][k]
            block = jnp.concatenate(
                [gf[core, h, 256 * k : 256 * k + 256] for h in (0, 1)], axis=1
            )
            square = jnp.sum(jnp.sum(block * block, axis=0, keepdims=True), axis=1, keepdims=True)
            norm = norm + 2.0 * square
            high, low = split(block)
            gc[b, 256 * a : 256 * a + 256] = block
            gch[256 * a : 256 * a + 256, 256 * b : 256 * b + 256] = high
            gcl[256 * a : 256 * a + 256, 256 * b : 256 * b + 256] = low
            block = block.T
            high, low = split(block)
            gc[a, 256 * b : 256 * b + 256] = block
            gch[256 * b : 256 * b + 256, 256 * a : 256 * a + 256] = high
            gcl[256 * b : 256 * b + 256, 256 * a : 256 * a + 256] = low
    factor = 2.0 / jnp.sqrt(norm + jnp.float32(1e-06))

    row = lax.broadcasted_iota(jnp.int32, (1024, 256), 0)
    col = lax.broadcasted_iota(jnp.int32, (1024, 256), 1)
    va[...] = jnp.where(row == col + 256 * t, 1.0, 0.0)
    vb[...] = factor * gc[t] - va[...]
    acc[...] = coefs[0] * va[...] + coefs[1] * vb[...]
    older, newer = va, vb
    for degree in (2, 3, 4):
        high, low = split(newer[...])
        vh[...] = high
        vl[...] = low
        for i in range(4):
            rows = slice(256 * i, 256 * i + 256)
            image = product(gch[rows], gcl[rows], vh[...], vl[...])
            following = 2.0 * (factor * image - newer[rows]) - older[rows]
            acc[rows] = acc[rows] + coefs[degree] * following
            older[rows] = following
        older, newer = newer, older

    for copy, _, there in rest[early:]:
        pl.when(there)(copy.wait_recv)
    for a in range(4):
        high, low = split(wf[a])
        wfh[:, 256 * a : 256 * a + 256] = high
        wfl[:, 256 * a : 256 * a + 256] = low
    high, low = split(acc[...])
    vh[...] = high
    vl[...] = low
    for i in range(2):
        rows = slice(256 * i, 256 * i + 256)
        lowrank = product(wfh[rows], wfl[rows], vh[...], vl[...])
        low_out[rows] = 0.5 * lowrank
    for copy in sent:
        copy.wait_send()
    for copy, here, _ in rest:
        pl.when(here)(copy.wait_send)


copies = 1 + 6 + 6 + 7 + 6 + 6 + 1 + 3 + 4 + 15 + 24 + 6 + 7 + 3 + 6 + 24 + 8


def on_device(telemetry, sparse, multiplier):
    block = jax.ShapeDtypeStruct((512, 256), f32)
    vmem = pl.BlockSpec(memory_space=pltpu.VMEM)
    half = pl.pallas_call(
        kernel,
        out_shape=block,
        in_specs=[pl.BlockSpec(memory_space=pltpu.HBM)] * 3,
        out_specs=vmem,
        scratch_shapes=[
            pltpu.VMEM((4, 512, 256), f32),
            pltpu.VMEM((4, 128, 256), f32),
            pltpu.VMEM((512, 256), bf16),
            pltpu.VMEM((512, 256), bf16),
            pltpu.VMEM((2, 256, 128), f32),
            pltpu.VMEM((2, 128, 128), f32),
            pltpu.VMEM((2, 3, 32, 128), f32),
            pltpu.VMEM((2, 32, 128), f32),
            pltpu.VMEM((2, 3, 8, 128), f32),
            pltpu.VMEM((2, 8, 128), f32),
            pltpu.VMEM((2, 4, 2, 8, 128), f32),
            pltpu.VMEM((2, 2, 16, 4, 8, 128), f32),
            pltpu.VMEM((4, 256, 256), bf16),
            pltpu.VMEM((4, 256, 256), bf16),
            pltpu.VMEM((2, 768, 128), f32),
            pltpu.VMEM((2, 3, 4, 48, 128), f32),
            pltpu.VMEM((2, 3, 48, 128), f32),
            pltpu.VMEM((2, 3, 48, 128), f32),
            pltpu.VMEM((96, 128), f32),
            pltpu.VMEM((2, 4, 24, 128), f32),
            pltpu.VMEM((96, 128), f32),
            pltpu.VMEM((2, 2, 768, 128), f32),
            pltpu.VMEM((4, 1024, 256), f32),
            pltpu.VMEM((1024, 1024), bf16),
            pltpu.VMEM((1024, 1024), bf16),
            pltpu.VMEM((1024, 256), f32),
            pltpu.VMEM((1024, 256), f32),
            pltpu.VMEM((1024, 256), bf16),
            pltpu.VMEM((1024, 256), bf16),
            pltpu.VMEM((1024, 256), f32),
            pltpu.VMEM((512, 1024), bf16),
            pltpu.VMEM((512, 1024), bf16),
            pltpu.VMEM((512, 256), f32),
            pltpu.VMEM((512, 256), f32),
            pltpu.VMEM((512, 256), f32),
            pltpu.SemaphoreType.DMA((3,)),
            pltpu.SemaphoreType.DMA((copies,)),
            pltpu.SemaphoreType.DMA((copies,)),
        ],
        compiler_params=pltpu.CompilerParams(
            collective_id=0, has_side_effects=True, vmem_limit_bytes=56 << 20
        ),
    )(telemetry, sparse, multiplier)
    lowrank = 2.0 * half
    level = telemetry - lowrank + multiplier
    size = jnp.maximum(jnp.abs(level) - shrink_level, 0.0)
    new_sparse = jnp.where(level < 0.0, -size, size)
    return lowrank, new_sparse, multiplier + telemetry - lowrank - new_sparse


def solution(mesh):
    spec = P("series", "tick")
    return jax.shard_map(
        on_device,
        mesh=mesh,
        in_specs=(spec, spec, spec),
        out_specs=(spec, spec, spec),
        check_vma=False,
    )
```
